32 devices in a mesh: fsdp: 32 (over z, y, x, core).
Axes of the slice: x: 2, y: 2, z: 4, core: 2. Of those that a mesh axis runs over, the one named last changes fastest.
Arguments:
- tokens: bfloat16 [4096, 1024], P('fsdp'), may hold values from -6 to 6
- lengths: int32 [32, 4], P('fsdp'), may hold values from 0 to 128, as said below
- cotangent: bfloat16 [4096, 1024], P('fsdp'), may hold values from -6 to 6
- w_in: bfloat16 [1024, 3352], P('fsdp'), may hold values from -0.1875 to 0.1875
- w_q: bfloat16 [1024, 512], P('fsdp'), may hold values from -0.1875 to 0.1875
- w_k: bfloat16 [1024, 128], P('fsdp'), may hold values from -0.1875 to 0.1875
- w_v: bfloat16 [1024, 128], P('fsdp'), may hold values from -0.1875 to 0.1875
- w_o: bfloat16 [512, 1024], P(None, 'fsdp'), may hold values from -2 to 2
- w_out: bfloat16 [1536, 1024], P(None, 'fsdp'), may hold values from -0.15625 to 0.15625
- w_gate: bfloat16 [1024, 2048], P('fsdp'), may hold values from -0.1875 to 0.1875
- w_up: bfloat16 [1024, 2048], P('fsdp'), may hold values from -0.1875 to 0.1875
- w_down: bfloat16 [2048, 1024], P(None, 'fsdp'), may hold values from -0.125 to 0.125
- gain_a: bfloat16 [1024], P('fsdp'), may hold values from 0.5 to 1.5
- gain_b: bfloat16 [1024], P('fsdp'), may hold values from 0.5 to 1.5
- conv_w: float32 [4, 1792], replicated, may hold values from -3 to 3
- conv_b: float32 [1792], replicated, may hold values from -3 to 3
- dt_bias: float32 [24], replicated, may hold values from -4 to -1
- a_log: float32 [24], replicated, may hold values from -4 to 1
- d_skip: float32 [24], replicated, may hold values from 0.5 to 1.5
Outputs:
- output: bfloat16 [4096, 1024], P('fsdp')
- d_tokens: bfloat16 [4096, 1024], P('fsdp')
- g_w_in: float32 [1024, 3352], P('fsdp')
- g_w_q: float32 [1024, 512], P('fsdp')
- g_w_k: float32 [1024, 128], P('fsdp')
- g_w_v: float32 [1024, 128], P('fsdp')
- g_w_o: float32 [512, 1024], P(None, 'fsdp')
- g_w_out: float32 [1536, 1024], P(None, 'fsdp')
- g_w_gate: float32 [1024, 2048], P('fsdp')
- g_w_up: float32 [1024, 2048], P('fsdp')
- g_w_down: float32 [2048, 1024], P(None, 'fsdp')
- g_gain_a: float32 [1024], P('fsdp')
- g_gain_b: float32 [1024], P('fsdp')
- g_conv_w: float32 [4, 1792], replicated
- g_conv_b: float32 [1792], replicated
- g_dt_bias: float32 [24], replicated
- g_a_log: float32 [24], replicated
- g_d_skip: float32 [24], replicated
The draws below stay inside these ranges and needn't reach their ends.
Inputs may be any that keep to these rules, and one draw needn't show every extreme that they name: Row p lists the lengths of the sequences on device p in order: nonzero entries come first, each 32 or more, and they sum to 128; zeros mark unused slots.
All inputs are finite; a program needn't handle non-finite values.
Results may differ from the reference program's by a relative error of at most 0.012.
Values may be sent and summed in bfloat16 or wider, within the bound.
A program may use at most 256 MiB of HBM per device.

```python
import jax
import jax.numpy as jnp
from jax import lax

D = 1024
FF = 2048
SSM_HEADS = 24
STATE = 128
CONVK = 4
Q_HEADS = 8
KV_HEADS = 2
HEAD_DIM = 64
TOK_DEV = 128
SLOTS = 4
MINLEN = 32
DSSM = 1536
CONV = 1792
DIN = 3352
QD = 512
KD = 128
TOKENS = 4096
N_FSDP = 32


def draw_lengths(key, part):
    key = jax.random.fold_in(key, 7)
    key_count, key_lone, key_cuts = jax.random.split(key, 3)
    slot_counts = jax.random.randint(key_count, (N_FSDP,), 1, SLOTS + 1)
    lone_device = jax.random.randint(key_lone, (), 0, N_FSDP)
    slot_counts = jnp.where(jnp.arange(N_FSDP) == lone_device, 1, slot_counts)
    spare_rows = TOK_DEV - SLOTS * MINLEN
    cut_points = jnp.sort(jax.random.randint(key_cuts, (N_FSDP, SLOTS - 1), 0, spare_rows + 1), axis=1)
    edge_points = jnp.concatenate([jnp.zeros((N_FSDP, 1), jnp.int32), cut_points.astype(jnp.int32), jnp.full((N_FSDP, 1), spare_rows, jnp.int32)], axis=1)
    extra_rows = edge_points[:, 1:] - edge_points[:, :-1]
    slot_index = jnp.arange(SLOTS)[None, :]
    active_slot = slot_index < slot_counts[:, None]
    seq_lengths = jnp.where(active_slot, MINLEN + extra_rows, 0)
    left_rows = TOK_DEV - jnp.sum(seq_lengths, axis=1, keepdims=True)
    seq_lengths = seq_lengths + jnp.where(slot_index == slot_counts[:, None] - 1, left_rows, 0)
    return seq_lengths.astype(jnp.int32)


def block_levels(key, extent, cuts, smallest, high):
    def one(dim, blocks):
        heights = jax.random.uniform(jax.random.fold_in(jax.random.fold_in(key, 6), dim), (blocks,), jnp.float32, smallest / len(cuts), high / len(cuts))
        return jnp.repeat(jnp.exp(heights), extent[dim] // blocks).reshape((-1,) + (1,) * (len(extent) - dim - 1))

    gain = one(*cuts[0])
    for cut in cuts[1:]:
        gain = gain * one(*cut)
    return gain


def scatter_about(own_key, dims, width, most, shards=(), kind=jnp.bfloat16):
    factor_of = block_levels(own_key, dims, shards, -0.22, 0.18) if shards else 1.0
    entries = jax.random.normal(own_key, dims, jnp.float32) * width * factor_of
    return jnp.minimum(jnp.maximum(entries, -most), most).astype(kind)


def setup_inputs(seed: int = 0) -> dict:
    streams_of = jax.random.split(jax.random.key(seed), 20)
    return {
        "tokens": scatter_about(streams_of[0], (TOKENS, D), 1.0, 6.0, ((0, 32),)),
        "lengths": draw_lengths(jax.random.fold_in(streams_of[19], 71), 0),
        "cotangent": scatter_about(streams_of[2], (TOKENS, D), 1.0, 6.0, ((0, 32),)),
        "w_in": scatter_about(streams_of[3], (D, DIN), D ** -0.5, 0.1875, ((0, 32),)),
        "w_q": scatter_about(streams_of[4], (D, QD), D ** -0.5, 0.1875, ((0, 32),)),
        "w_k": scatter_about(streams_of[5], (D, KD), D ** -0.5, 0.1875, ((0, 32),)),
        "w_v": scatter_about(streams_of[6], (D, KD), D ** -0.5, 0.1875, ((0, 32),)),
        "w_o": scatter_about(streams_of[7], (QD, D), (max(QD // 64, 1)) ** -0.5, 2.0, ((1, 32),)),
        "w_out": scatter_about(streams_of[8], (DSSM, D), DSSM ** -0.5, 0.15625, ((1, 32),)),
        "w_gate": scatter_about(streams_of[9], (D, FF), D ** -0.5, 0.1875, ((0, 32),)),
        "w_up": scatter_about(streams_of[10], (D, FF), D ** -0.5, 0.1875, ((0, 32),)),
        "w_down": scatter_about(streams_of[11], (FF, D), FF ** -0.5, 0.125, ((1, 32),)),
        "gain_a": jnp.clip(1.0 + 0.1 * jax.random.normal(streams_of[12], (D,), jnp.float32), 0.5, 1.5).astype(jnp.bfloat16),
        "gain_b": jnp.clip(1.0 + 0.1 * jax.random.normal(streams_of[13], (D,), jnp.float32), 0.5, 1.5).astype(jnp.bfloat16),
        "conv_w": scatter_about(streams_of[14], (CONVK, CONV), CONVK ** -0.5, 3.0, (), jnp.float32),
        "conv_b": scatter_about(streams_of[15], (CONV,), 0.5, 3.0, (), jnp.float32),
        "dt_bias": jnp.clip(jax.random.uniform(streams_of[16], (SSM_HEADS,), jnp.float32, -4.0, -1.0), -4.0, -1.0),
        "a_log": jnp.clip(jax.random.uniform(streams_of[17], (SSM_HEADS,), jnp.float32, -4.0, 1.0), -4.0, 1.0),
        "d_skip": jnp.clip(jax.random.uniform(streams_of[18], (SSM_HEADS,), jnp.float32, 0.5, 1.5), 0.5, 1.5),
    }


norm_eps = 1e-05
rope_base = 100000000000.0
highest = lax.Precision.HIGHEST

@jax.custom_vjp
def low(v):
    return lax.optimization_barrier(v.astype(jnp.bfloat16)).astype(jnp.float32)

@jax.custom_vjp
def low_back(v):
    return v

def low_keep(v):
    return (low(v), None)

def low_pass(kept, grad):
    return (grad,)

def back_keep(v):
    return (v, None)

def back_low(kept, grad):
    return (low(grad),)
low.defvjp(low_keep, low_pass)
low_back.defvjp(back_keep, back_low)

def segment_layout(lengths_row, row_count):
    seq_ends = jnp.cumsum(lengths_row).astype(jnp.int32)
    seq_starts = (seq_ends - lengths_row).astype(jnp.int32)
    places = jnp.arange(row_count, dtype=jnp.int32)
    segment = lax.optimization_barrier(jnp.sum((places[:, None] >= seq_ends[None, :]).astype(jnp.int32), axis=1))
    picked = (segment[:, None] == jnp.arange(lengths_row.shape[0], dtype=jnp.int32)[None, :]).astype(jnp.int32)
    position = places - lax.optimization_barrier(jnp.sum(picked * seq_starts[None, :], axis=1))
    return (segment, position)

def rms_scaled(values, gain_row):
    return values * lax.rsqrt(lax.optimization_barrier(jnp.mean(values * values, axis=1, keepdims=True)) + norm_eps) * gain_row[None, :]

def rotate(values, position):
    half_dim = values.shape[-1] // 2
    ladder = jnp.arange(half_dim, dtype=jnp.float32) * (-2.0 / values.shape[-1])
    inverse = jnp.power(jnp.float32(rope_base), ladder)
    angles = position.astype(jnp.float32)[:, None] * inverse[None, :]
    cosine = jnp.cos(angles)[:, None, :]
    sine_rows = jnp.sin(angles)[:, None, :]
    half_one = values[..., :half_dim]
    second = values[..., half_dim:]
    return jnp.concatenate([half_one * cosine - second * sine_rows, second * cosine + half_one * sine_rows], axis=-1)

def causal_conv(xbc_in, segment, conv_weight, conv_bias):
    row_count = xbc_in.shape[0]
    taps = conv_weight.shape[0]
    conv_sum = jnp.zeros_like(xbc_in) + conv_bias[None, :]
    for tap_index in range(taps):
        lag_rows = taps - 1 - tap_index
        shifted = jnp.pad(xbc_in, ((lag_rows, 0), (0, 0)))[:row_count]
        seg_shift = jnp.pad(segment, (lag_rows, 0), constant_values=-1)[:row_count]
        keep_rows = (seg_shift == segment).astype(xbc_in.dtype)
        conv_sum = conv_sum + conv_weight[tap_index][None, :] * shifted * keep_rows[:, None]
    return conv_sum

def mamba_inputs(xbc_in, dt_in, segment, conv_weight, conv_bias, dt_shift, a_logs):
    activated = jax.nn.silu(causal_conv(xbc_in, segment, conv_weight, conv_bias))
    row_count = xbc_in.shape[0]
    head_count = dt_shift.shape[0]
    x_heads = activated[:, :DSSM].reshape(row_count, head_count, DSSM // head_count)
    b_state = activated[:, DSSM:DSSM + STATE]
    c_state = activated[:, DSSM + STATE:]
    dt_step = jax.nn.softplus(dt_in + dt_shift[None, :])
    log_decay = -jnp.exp(a_logs)[None, :] * dt_step
    running = jnp.cumsum(log_decay, axis=0).T
    places = jnp.arange(row_count)
    causal = (segment[:, None] == segment[None, :]) & (places[:, None] >= places[None, :])
    gap_log = running[:, :, None] - running[:, None, :]
    decay_mask = jnp.exp(jnp.where(causal[None], gap_log, -10000.0))
    return (x_heads, b_state, c_state, dt_step, decay_mask)

def block_mix(zxd, q_raw, k_raw, v_raw, lengths_row, conv_w, conv_b, dt_bias, a_log, d_skip):
    row_count = zxd.shape[0]
    segment, position = segment_layout(lengths_row, row_count)
    z_gate = zxd[:, :DSSM]
    xbc_in = zxd[:, DSSM:DSSM + CONV]
    dt_raw = zxd[:, DSSM + CONV:]
    x_heads, b_state, c_state, dt_step, decay_mask = mamba_inputs(xbc_in, dt_raw, segment, conv_w, conv_b, dt_bias, a_log)
    gram_cb = low_back(jnp.dot(low(c_state), low(b_state).T, precision=highest))
    mix_low = low(gram_cb[None] * decay_mask)
    vals_low = low(dt_step[:, :, None] * x_heads)
    y_heads = low_back(jnp.einsum('hts,shp->thp', mix_low, vals_low, precision=highest))
    y_flat = (y_heads + d_skip[None, :, None] * x_heads).reshape(row_count, DSSM)
    gated_low = low(y_flat * jax.nn.silu(z_gate))
    q_rot = low(rotate(q_raw.reshape(row_count, Q_HEADS, HEAD_DIM), position))
    k_rot = low(rotate(k_raw.reshape(row_count, KV_HEADS, HEAD_DIM), position))
    group_size = Q_HEADS // KV_HEADS
    q_group = q_rot.reshape(row_count, KV_HEADS, group_size, HEAD_DIM)
    v_group = v_raw.reshape(row_count, KV_HEADS, HEAD_DIM)
    raw_scores = jnp.einsum('tkgd,skd->kgts', q_group, k_rot, precision=highest) * HEAD_DIM ** (-0.5)
    score_rows = low_back(raw_scores)
    places = jnp.arange(row_count)
    causal = (segment[:, None] == segment[None, :]) & (places[:, None] >= places[None, :])
    masked = jnp.where(causal[None, None], score_rows, -1000000000.0)
    row_peak = lax.optimization_barrier(jnp.max(masked, axis=-1, keepdims=True))
    exp_rows = jnp.exp(masked - row_peak)
    prob_rows = low(exp_rows / lax.optimization_barrier(jnp.sum(exp_rows, axis=-1, keepdims=True)))
    attended = jnp.einsum('kgts,skd->tkgd', prob_rows, v_group, precision=highest)
    context = low(low_back(attended)).reshape(row_count, QD)
    return (gated_low, context)

def layer(tokens, w_in, w_q, w_k, w_v, w_o, w_out, w_gate, w_up, w_down, gain_a, gain_b, conv_w, conv_b, dt_bias, a_log, d_skip, lengths):
    normed = low(rms_scaled(tokens, gain_a))
    zxd = low_back(jnp.dot(normed, w_in, precision=highest))
    q_raw = low_back(jnp.dot(normed, w_q, precision=highest))
    k_raw = low_back(jnp.dot(normed, w_k, precision=highest))
    v_raw = low(low_back(jnp.dot(normed, w_v, precision=highest)))

    def one_block(pieces):
        return block_mix(pieces[0], pieces[1], pieces[2], pieces[3], pieces[4], conv_w, conv_b, dt_bias, a_log, d_skip)
    stacked = (zxd.reshape(N_FSDP, TOK_DEV, DIN), q_raw.reshape(N_FSDP, TOK_DEV, QD), k_raw.reshape(N_FSDP, TOK_DEV, KD), v_raw.reshape(N_FSDP, TOK_DEV, KD), lengths)
    gated_all, context_all = lax.map(jax.checkpoint(one_block), stacked)
    gated_all = gated_all.reshape(TOKENS, DSSM)
    context_all = context_all.reshape(TOKENS, QD)
    attn_out = low_back(jnp.dot(context_all, w_o, precision=highest))
    mamba_out = low_back(jnp.dot(gated_all, w_out, precision=highest))
    mid_sum = tokens + attn_out + mamba_out
    normed_b = low(rms_scaled(mid_sum, gain_b))
    gate_pre = low_back(jnp.dot(normed_b, w_gate, precision=highest))
    upward = low_back(jnp.dot(normed_b, w_up, precision=highest))
    hidden = low(jax.nn.silu(gate_pre) * upward)
    return mid_sum + low_back(jnp.dot(hidden, w_down, precision=highest))

def reference(tokens, lengths, cotangent, w_in, w_q, w_k, w_v, w_o, w_out, w_gate, w_up, w_down, gain_a, gain_b, conv_w, conv_b, dt_bias, a_log, d_skip):
    initials = (tokens, w_in, w_q, w_k, w_v, w_o, w_out, w_gate, w_up, w_down, gain_a, gain_b, conv_w, conv_b, dt_bias, a_log, d_skip)
    floats = tuple((array_in.astype(jnp.float32) for array_in in initials))

    def layer_fixed(*arrays):
        return layer(*arrays, lengths)
    result, pullback = jax.vjp(layer_fixed, *floats)
    gradients = pullback(cotangent.astype(jnp.float32))
    return (result.astype(jnp.bfloat16), gradients[0].astype(jnp.bfloat16), gradients[1], gradients[2], gradients[3], gradients[4], gradients[5], gradients[6], gradients[7], gradients[8], gradients[9], gradients[10], gradients[11], gradients[12], gradients[13], gradients[14], gradients[15], gradients[16])
```

```python
import jax
import jax.numpy as jnp
from jax import lax
from jax.experimental import pallas as pl
from jax.experimental.pallas import tpu as pltpu
from jax.sharding import PartitionSpec as P

FF = 2048
STATE = 128
Q_HEADS = 8
KV_HEADS = 2
HEAD_DIM = 64
DSSM = 1536
CONV = 1792
DIN = 3352
QD = 512
KD = 128


norm_eps = 1e-05
rope_base = 100000000000.0


def segment_layout(lengths_row, row_count):
    seq_ends = jnp.cumsum(lengths_row)
    seq_starts = seq_ends - lengths_row
    places = jnp.arange(row_count, dtype=jnp.int32)
    segment = jnp.sum((places[:, None] >= seq_ends[None, :]).astype(jnp.int32), axis=1)
    picked = (
        segment[:, None] == jnp.arange(lengths_row.shape[0], dtype=jnp.int32)[None, :]
    ).astype(jnp.int32)
    position = places - jnp.sum(picked * seq_starts[None, :], axis=1)
    return (segment, position)


def rms_scaled(values, gain_row):
    return (
        values
        * lax.rsqrt(jnp.mean(values * values, axis=1, keepdims=True) + norm_eps)
        * gain_row[None, :]
    )


def rotate(values, position):
    half_dim = values.shape[-1] // 2
    ladder = jnp.arange(half_dim, dtype=jnp.float32) * (-2.0 / values.shape[-1])
    inverse = jnp.power(jnp.float32(rope_base), ladder)
    angles = position.astype(jnp.float32)[:, None] * inverse[None, :]
    cosine = jnp.cos(angles)[:, None, :]
    sine_rows = jnp.sin(angles)[:, None, :]
    half_one = values[..., :half_dim]
    second = values[..., half_dim:]
    return jnp.concatenate(
        [half_one * cosine - second * sine_rows, second * cosine + half_one * sine_rows], axis=-1
    )


def causal_conv(xbc_in, segment, conv_weight, conv_bias):
    row_count = xbc_in.shape[0]
    taps = conv_weight.shape[0]
    conv_sum = jnp.zeros_like(xbc_in) + conv_bias[None, :]
    for tap_index in range(taps):
        lag_rows = taps - 1 - tap_index
        shifted = jnp.pad(xbc_in, ((lag_rows, 0), (0, 0)))[:row_count]
        seg_shift = jnp.pad(segment, (lag_rows, 0), constant_values=-1)[:row_count]
        keep_rows = (seg_shift == segment).astype(xbc_in.dtype)
        conv_sum = conv_sum + conv_weight[tap_index][None, :] * shifted * keep_rows[:, None]
    return conv_sum


def mamba_inputs(xbc_in, dt_in, segment, conv_weight, conv_bias, dt_shift, a_logs):
    activated = jax.nn.silu(causal_conv(xbc_in, segment, conv_weight, conv_bias))
    row_count = xbc_in.shape[0]
    head_count = dt_shift.shape[0]
    x_heads = activated[:, :DSSM].reshape(row_count, head_count, DSSM // head_count)
    b_state = activated[:, DSSM : DSSM + STATE]
    c_state = activated[:, DSSM + STATE :]
    dt_step = jax.nn.softplus(dt_in + dt_shift[None, :])
    log_decay = -jnp.exp(a_logs)[None, :] * dt_step
    running = jnp.cumsum(log_decay, axis=0).T
    places = jnp.arange(row_count)
    causal = (segment[:, None] == segment[None, :]) & (places[:, None] >= places[None, :])
    gap_log = running[:, :, None] - running[:, None, :]
    decay_mask = jnp.exp(jnp.where(causal[None], gap_log, -10000.0))
    return (x_heads, b_state, c_state, dt_step, decay_mask)


def gated_out(y_heads, x_heads, z_gate, skip_rates):
    row_count = y_heads.shape[0]
    y_flat = (y_heads + skip_rates[None, :, None] * x_heads).reshape(row_count, -1)
    return y_flat * jax.nn.silu(z_gate)


def swiglu(gate_pre, upward):
    return jax.nn.silu(gate_pre) * upward


def forward_prod(rows_in, weight):
    return jnp.dot(rows_in, weight, preferred_element_type=jnp.float32)


def outer_sum(left_rows, right_rows):
    return lax.dot_general(
        left_rows, right_rows, (((0,), (0,)), ((), ())), preferred_element_type=jnp.float32
    )


def back_prod(grad_rows, weight):
    return lax.dot_general(
        grad_rows, weight, (((1,), (1,)), ((), ())), preferred_element_type=jnp.float32
    )


MESH = pl.DeviceIdType.MESH
IN_PAD = 3456
PROJ = IN_PAD + QD + 2 * KD
GATHER_CHUNKS = ((0, 0, 2176), (0, 2176, 2176), (1, 0, 2048), (2, 0, 2048), (2, 2048, 2048), (3, 0, 2048))
REDUCE_CHUNKS = ((3, 0, 2048), (2, 0, 2048), (2, 2048, 2048), (1, 0, 2048), (0, 0, 2176), (0, 2176, 2048))


def place_of(me):
    return me // 8, (me // 4) % 2, (me // 2) % 2, me % 2


def index_of(z, y, x, core):
    return ((z * 2 + y) * 2 + x) * 2 + core


def enter(depth, z, y, x, core):
    barrier = pltpu.get_barrier_semaphore()
    partners = [
        index_of(z, y, x, 1 - core),
        index_of(z, y, 1 - x, core),
        index_of(z, 1 - y, x, core),
    ] + [index_of((z + j) % depth, y, x, core) for j in range(1, depth)]
    for partner in partners:
        pl.semaphore_signal(barrier, inc=1, device_id=(partner,), device_id_type=MESH)
    pl.semaphore_wait(barrier, len(partners))


def gather_kernel(depth, *refs):
    count = len(GATHER_CHUNKS)
    shards, fulls = refs[:4], refs[4:8]
    own_sem, z_send, z_recv, p_send, p_recv, c_send, c_recv = refs[8:]
    z, y, x, core = place_of(lax.axis_index("fsdp"))
    sibling = index_of(z, y, x, 1 - core)
    enter(depth, z, y, x, core)

    def remote(src, dst, send, recv, device):
        return pltpu.make_async_remote_copy(
            src_ref=src,
            dst_ref=dst,
            send_sem=send,
            recv_sem=recv,
            device_id=(device,),
            device_id_type=MESH,
        )

    own_copies, z_copies = [], []
    for c, (which, first, width) in enumerate(GATHER_CHUNKS):
        cols = pl.ds(first, width)
        mine = shards[which].at[:, cols]
        spot = fulls[which].at[z, y, x, core, :, cols]
        row = []
        for j in range(1, depth):
            copy = remote(
                mine,
                spot,
                z_send.at[c, j - 1],
                z_recv.at[c, j - 1],
                index_of((z + j) % depth, y, x, core),
            )
            copy.start()
            row.append(copy)
        z_copies.append(row)
        own = pltpu.make_async_copy(mine, spot, own_sem.at[c])
        own.start()
        own_copies.append(own)

    sent = []

    def region(c, ys, xs, co):
        which, first, width = GATHER_CHUNKS[c]
        return fulls[which].at[:, ys, xs, co, :, pl.ds(first, width)]

    def to_sibling(c, step, ys, xs):
        src = region(c, ys, xs, core)
        copy = remote(src, src, c_send.at[c, step], c_recv.at[c, step], sibling)
        copy.start()
        sent.append(copy)

    def step_one(c):
        which, first, width = GATHER_CHUNKS[c]
        for j in range(1, depth):
            spot = fulls[which].at[(z + depth - j) % depth, y, x, core, :, pl.ds(first, width)]
            remote(spot, spot, z_send.at[c, j - 1], z_recv.at[c, j - 1], sibling).wait_recv()
        own_copies[c].wait()
        src = region(c, y, x, core)
        other = index_of(z, y, 1 - x, core) if c % 2 == 0 else index_of(z, 1 - y, x, core)
        copy = remote(src, src, p_send.at[c, 0], p_recv.at[c, 0], other)
        copy.start()
        sent.append(copy)
        to_sibling(c, 0, y, x)

    def step_two(c):
        if c % 2 == 0:
            spot = region(c, y, 1 - x, core)
            src = region(c, y, slice(None), core)
            other = index_of(z, 1 - y, x, core)
        else:
            spot = region(c, 1 - y, x, core)
            src = region(c, slice(None), x, core)
            other = index_of(z, y, 1 - x, core)
        remote(spot, spot, p_send.at[c, 0], p_recv.at[c, 0], sibling).wait_recv()
        copy = remote(src, src, p_send.at[c, 1], p_recv.at[c, 1], other)
        copy.start()
        sent.append(copy)
        if c % 2 == 0:
            to_sibling(c, 1, y, 1 - x)
        else:
            to_sibling(c, 1, 1 - y, x)

    def step_three(c):
        if c % 2 == 0:
            ys, xs = 1 - y, slice(None)
        else:
            ys, xs = slice(None), 1 - x
        spot = region(c, ys, xs, core)
        remote(spot, spot, p_send.at[c, 1], p_recv.at[c, 1], sibling).wait_recv()
        to_sibling(c, 2, ys, xs)

    for t in range(count + 2):
        if t < count:
            step_one(t)
        if 0 <= t - 1 < count:
            step_two(t - 1)
        if 0 <= t - 2 < count:
            step_three(t - 2)
    for c in range(count):
        if c % 2 == 0:
            parts = ((y, x), (y, 1 - x), (1 - y, slice(None)))
        else:
            parts = ((y, x), (1 - y, x), (slice(None), 1 - x))
        for step, (ys, xs) in enumerate(parts):
            spot = region(c, ys, xs, 1 - core)
            remote(spot, spot, c_send.at[c, step], c_recv.at[c, step], sibling).wait_recv()
    for row in z_copies:
        for copy in row:
            copy.wait_send()
    for copy in sent:
        copy.wait_send()


def gather_fast(shards, n):
    depth = n // 8
    rows = shards[0].shape[0]
    count = len(GATHER_CHUNKS)
    anywhere = pl.BlockSpec(memory_space=pl.ANY)
    dma = pltpu.SemaphoreType.DMA
    fulls = pl.pallas_call(
        lambda *refs: gather_kernel(depth, *refs),
        out_shape=tuple(
            jax.ShapeDtypeStruct((depth, 2, 2, 2, rows, s.shape[1]), s.dtype) for s in shards
        ),
        in_specs=[anywhere] * 4,
        out_specs=(anywhere,) * 4,
        scratch_shapes=[
            dma((count,)),
            dma((count, depth - 1)),
            dma((count, depth - 1)),
            dma((count, 2)),
            dma((count, 2)),
            dma((count, 3)),
            dma((count, 3)),
        ],
        compiler_params=pltpu.CompilerParams(collective_id=0, has_side_effects=True),
        name="gather_weights",
    )(*shards)
    return tuple(f.reshape(n * rows, f.shape[-1]) for f in fulls)


def reduce_kernel(depth, *refs):
    count = len(REDUCE_CHUNKS)
    grads, small = refs[:4], refs[4]
    outs, small_out = refs[5:9], refs[9]
    rest = list(refs[10:])
    held = rest[:count]
    c_buf = rest[count : 2 * count]
    one_buf = rest[2 * count : 3 * count]
    two_buf = rest[3 * count : 4 * count]
    z_buf = rest[4 * count : 5 * count]
    (s_cur, s_buf, s_z, own_sem, c_send, c_recv, p_send, p_recv, z_send, z_recv,
     s_send, s_recv, sz_send, sz_recv) = rest[5 * count :]
    z, y, x, core = place_of(lax.axis_index("fsdp"))
    sibling = index_of(z, y, x, 1 - core)
    beside_x = index_of(z, y, 1 - x, core)
    beside_y = index_of(z, 1 - y, x, core)
    enter(depth, z, y, x, core)

    def remote(src, dst, send, recv, device):
        return pltpu.make_async_remote_copy(
            src_ref=src,
            dst_ref=dst,
            send_sem=send,
            recv_sem=recv,
            device_id=(device,),
            device_id_type=MESH,
        )

    core_copies, own_copies, sent = [], [], []
    for c, (which, first, width) in enumerate(REDUCE_CHUNKS):
        cols = pl.ds(first, width)
        copy = remote(
            grads[which].at[:, :, :, 1 - core, :, cols],
            c_buf[c],
            c_send.at[c],
            c_recv.at[c],
            sibling,
        )
        copy.start()
        core_copies.append(copy)
        own = pltpu.make_async_copy(
            grads[which].at[:, :, :, core, :, cols], held[c], own_sem.at[c]
        )
        own.start()
        own_copies.append(own)

    def summed(first, second):
        return (first.astype(jnp.float32) + second.astype(jnp.float32)).astype(jnp.bfloat16)

    def step_core(c):
        own_copies[c].wait()
        core_copies[c].wait_recv()

        def add(i, carry):
            a, b, d = i // 4, (i // 2) % 2, i % 2
            held[c][a, b, d] = summed(held[c][a, b, d], c_buf[c][a, b, d])
            return carry

        lax.fori_loop(0, depth * 4, add, 0)
        if c % 2 == 0:
            copy = remote(
                held[c].at[:, 1 - y], one_buf[c], p_send.at[c, 0], p_recv.at[c, 0], beside_y
            )
        else:
            copy = remote(
                held[c].at[:, :, 1 - x], one_buf[c], p_send.at[c, 0], p_recv.at[c, 0], beside_x
            )
        copy.start()
        sent.append(copy)

    def step_one(c):
        remote(one_buf[c], one_buf[c], p_send.at[c, 0], p_recv.at[c, 0], sibling).wait_recv()

        def add(i, carry):
            a, b = i // 2, i % 2
            if c % 2 == 0:
                held[c][a, y, b] = summed(held[c][a, y, b], one_buf[c][a, b])
            else:
                held[c][a, b, x] = summed(held[c][a, b, x], one_buf[c][a, b])
            return carry

        lax.fori_loop(0, depth * 2, add, 0)
        if c % 2 == 0:
            src, other = held[c].at[:, y, 1 - x], beside_x
        else:
            src, other = held[c].at[:, 1 - y, x], beside_y
        copy = remote(src, two_buf[c], p_send.at[c, 1], p_recv.at[c, 1], other)
        copy.start()
        sent.append(copy)

    def step_two(c):
        remote(two_buf[c], two_buf[c], p_send.at[c, 1], p_recv.at[c, 1], sibling).wait_recv()

        def add(a, carry):
            held[c][a, y, x] = summed(held[c][a, y, x], two_buf[c][a])
            return carry

        lax.fori_loop(0, depth, add, 0)
        for j in range(1, depth):
            to = (z + j) % depth
            copy = remote(
                held[c].at[to, y, x],
                z_buf[c].at[j - 1],
                z_send.at[c, j - 1],
                z_recv.at[c, j - 1],
                index_of(to, y, x, core),
            )
            copy.start()
            sent.append(copy)

    def step_z(c):
        which, first, width = REDUCE_CHUNKS[c]
        total = held[c][z, y, x].astype(jnp.float32)
        for j in range(1, depth):
            spot = z_buf[c].at[j - 1]
            remote(spot, spot, z_send.at[c, j - 1], z_recv.at[c, j - 1], sibling).wait_recv()
            total = total + z_buf[c][j - 1].astype(jnp.float32)
        outs[which][:, first : first + width] = total

    small_sent = []

    def small_start(step):
        if step == 0:
            s_cur[...] = small[...]
        if step < 3:
            copy = remote(
                s_cur,
                s_buf.at[step],
                s_send.at[step],
                s_recv.at[step],
                (sibling, beside_x, beside_y)[step],
            )
            copy.start()
            small_sent.append(copy)
        else:
            s_z[z] = s_cur[...]
            for j in range(1, depth):
                copy = remote(
                    s_cur,
                    s_z.at[z],
                    sz_send.at[j - 1],
                    sz_recv.at[j - 1],
                    index_of((z + j) % depth, y, x, core),
                )
                copy.start()
                sent.append(copy)

    def small_end(step):
        if step < 3:
            small_sent[step].wait()
            s_cur[...] = s_cur[...] + s_buf[step]
        else:
            for j in range(1, depth):
                spot = s_z.at[(z + depth - j) % depth]
                remote(spot, spot, sz_send.at[j - 1], sz_recv.at[j - 1], sibling).wait_recv()
            total = s_z[0]
            for a in range(1, depth):
                total = total + s_z[a]
            small_out[...] = total

    small_start(0)
    for t in range(count + 3):
        if t < count:
            step_core(t)
        if 0 <= t - 1 < count:
            step_one(t - 1)
        if 0 <= t - 2 < count:
            step_two(t - 2)
        if 0 <= t - 3 < count:
            step_z(t - 3)
        if t < 4:
            small_end(t)
        if t < 3:
            small_start(t + 1)
    for copy in core_copies:
        copy.wait_send()
    for copy in sent:
        copy.wait_send()


def reduce_fast(grads, small, n):
    depth = n // 8
    rows = grads[0].shape[0] // n
    count = len(REDUCE_CHUNKS)
    anywhere = pl.BlockSpec(memory_space=pl.ANY)
    vmem = pl.BlockSpec(memory_space=pltpu.VMEM)
    dma = pltpu.SemaphoreType.DMA
    blocks = [g.reshape(depth, 2, 2, 2, rows, g.shape[1]) for g in grads]
    widths = [width for (_, _, width) in REDUCE_CHUNKS]

    def buffers(*lead):
        return [pltpu.VMEM(lead + (rows, width), jnp.bfloat16) for width in widths]

    return pl.pallas_call(
        lambda *refs: reduce_kernel(depth, *refs),
        out_shape=tuple(jax.ShapeDtypeStruct((rows, g.shape[1]), jnp.float32) for g in grads)
        + (jax.ShapeDtypeStruct(small.shape, jnp.float32),),
        in_specs=[anywhere] * 4 + [vmem],
        out_specs=(vmem,) * 5,
        scratch_shapes=buffers(depth, 2, 2)
        + buffers(depth, 2, 2)
        + buffers(depth, 2)
        + buffers(depth)
        + buffers(depth - 1)
        + [
            pltpu.VMEM(small.shape, jnp.float32),
            pltpu.VMEM((3,) + small.shape, jnp.float32),
            pltpu.VMEM((depth,) + small.shape, jnp.float32),
            dma((count,)),
            dma((count,)),
            dma((count,)),
            dma((count, 2)),
            dma((count, 2)),
            dma((count, depth - 1)),
            dma((count, depth - 1)),
            dma((3,)),
            dma((3,)),
            dma((depth - 1,)),
            dma((depth - 1,)),
        ],
        compiler_params=pltpu.CompilerParams(
            collective_id=1, has_side_effects=True, vmem_limit_bytes=52 * 1024 * 1024
        ),
        name="reduce_grads",
    )(*blocks, small)


def gather_weights(shards, n):
    if n == 32:
        return gather_fast(shards, n)
    return tuple(lax.all_gather(s, "fsdp", axis=0, tiled=True) for s in shards)


def reduce_grads(grads, small, n):
    if n == 32:
        return reduce_fast(grads, small, n)
    summed = [
        lax.psum_scatter(g.astype(jnp.float32), "fsdp", scatter_dimension=0, tiled=True)
        for g in grads
    ]
    return (*summed, lax.psum(small, "fsdp"))


def per_device(
    tokens,
    lengths,
    cotangent,
    w_in,
    w_q,
    w_k,
    w_v,
    w_o,
    w_out,
    w_gate,
    w_up,
    w_down,
    gain_a,
    gain_b,
    conv_w,
    conv_b,
    dt_bias,
    a_log,
    d_skip,
):
    n = lax.axis_size("fsdp")
    rows = w_in.shape[0]

    def blank(columns):
        return jnp.zeros((rows, columns), jnp.bfloat16)

    shards = (
        jnp.concatenate(
            [
                w_in,
                blank(IN_PAD - DIN),
                w_q,
                w_k,
                w_v,
                gain_a[:, None],
                gain_b[:, None],
                blank(126),
            ],
            axis=1,
        ),
        jnp.concatenate([w_o.T, w_out.T], axis=1),
        jnp.concatenate([w_gate, w_up], axis=1),
        w_down.T,
    )
    full_proj, full_mixed, full_glu, full_down = gather_weights(shards, n)
    full_ga = full_proj[:, PROJ]
    full_gb = full_proj[:, PROJ + 1]
    row_count = tokens.shape[0]
    segment, position = segment_layout(lengths[0], row_count)
    places = jnp.arange(row_count)
    causal = (segment[:, None] == segment[None, :]) & (places[:, None] >= places[None, :])
    resid_in = tokens.astype(jnp.float32)
    normed_f, norm_back_a = jax.vjp(rms_scaled, resid_in, full_ga.astype(jnp.float32))
    normed = normed_f.astype(jnp.bfloat16)
    projected = forward_prod(normed, full_proj)
    zxd = projected[:, :DIN]
    q_raw = projected[:, IN_PAD : IN_PAD + QD]
    k_raw = projected[:, IN_PAD + QD : IN_PAD + QD + KD]
    v_low = projected[:, IN_PAD + QD + KD : PROJ].astype(jnp.bfloat16)
    z_gate = zxd[:, :DSSM]
    xbc_in = zxd[:, DSSM : DSSM + CONV]
    dt_raw = zxd[:, DSSM + CONV :]

    def pre_part(xbc_part, dt_part, conv_weight, conv_bias, dt_shift, a_logs):
        return mamba_inputs(xbc_part, dt_part, segment, conv_weight, conv_bias, dt_shift, a_logs)

    (x_heads, b_state, c_state, dt_step, decay_mask), pre_back = jax.vjp(
        pre_part, xbc_in, dt_raw, conv_w, conv_b, dt_bias, a_log
    )
    b_low = b_state.astype(jnp.bfloat16)
    c_low = c_state.astype(jnp.bfloat16)
    gram_cb = lax.dot_general(
        c_low, b_low, (((1,), (1,)), ((), ())), preferred_element_type=jnp.float32
    )
    mix_low = (gram_cb[None] * decay_mask).astype(jnp.bfloat16)
    vals_low = (dt_step[:, :, None] * x_heads).astype(jnp.bfloat16)
    y_heads = jnp.einsum("hts,shp->thp", mix_low, vals_low, preferred_element_type=jnp.float32)
    gated_f, post_back = jax.vjp(gated_out, y_heads, x_heads, z_gate, d_skip)
    gated_low = gated_f.astype(jnp.bfloat16)

    def rope_pair(q_part, k_part):
        return (
            rotate(q_part.reshape(row_count, Q_HEADS, HEAD_DIM), position),
            rotate(k_part.reshape(row_count, KV_HEADS, HEAD_DIM), position),
        )

    (q_rot, k_rot), rope_back = jax.vjp(rope_pair, q_raw, k_raw)
    group_size = Q_HEADS // KV_HEADS
    q_low = q_rot.astype(jnp.bfloat16).reshape(row_count, KV_HEADS, group_size, HEAD_DIM)
    k_low = k_rot.astype(jnp.bfloat16)
    v_group = v_low.reshape(row_count, KV_HEADS, HEAD_DIM)
    score_scale = HEAD_DIM ** (-0.5)

    def masked_scores():
        raw_scores = (
            jnp.einsum("tkgd,skd->kgts", q_low, k_low, preferred_element_type=jnp.float32)
            * score_scale
        )
        return jnp.where(causal[None, None], raw_scores, -1000000000.0)

    masked = masked_scores()
    row_peak = jnp.max(masked, axis=-1, keepdims=True)
    row_total = jnp.sum(jnp.exp(masked - row_peak), axis=-1, keepdims=True)
    prob_rows = jnp.exp(masked - row_peak) / row_total
    attended = jnp.einsum(
        "kgts,skd->tkgd",
        prob_rows.astype(jnp.bfloat16),
        v_group,
        preferred_element_type=jnp.float32,
    )
    context = attended.astype(jnp.bfloat16).reshape(row_count, QD)
    mixed_outs = jnp.concatenate([context, gated_low], axis=1)
    mid_sum = resid_in + back_prod(mixed_outs, full_mixed)
    normed_bf, norm_back_b = jax.vjp(rms_scaled, mid_sum, full_gb.astype(jnp.float32))
    normed_b = normed_bf.astype(jnp.bfloat16)
    glu_pre = forward_prod(normed_b, full_glu)
    gate_pre = glu_pre[:, :FF]
    upward = glu_pre[:, FF:]
    hidden_f, glu_back = jax.vjp(swiglu, gate_pre, upward)
    hidden = hidden_f.astype(jnp.bfloat16)
    result = (mid_sum + back_prod(hidden, full_down)).astype(jnp.bfloat16)
    grad_top = cotangent.astype(jnp.float32)
    d_hidden = forward_prod(cotangent, full_down)
    d_gate_f, d_up_f = glu_back(d_hidden)
    d_gate = d_gate_f.astype(jnp.bfloat16)
    d_up = d_up_f.astype(jnp.bfloat16)
    d_glu = jnp.concatenate([d_gate, d_up], axis=1)
    d_normed_b = back_prod(d_glu, full_glu)
    d_mid_norm, g_gain_b = norm_back_b(d_normed_b)
    d_mid = grad_top + d_mid_norm
    d_branch = d_mid.astype(jnp.bfloat16)
    d_mixed = forward_prod(d_branch, full_mixed)
    d_context = d_mixed[:, :QD]
    d_gated = d_mixed[:, QD:]
    d_att_low = d_context.reshape(row_count, KV_HEADS, group_size, HEAD_DIM).astype(jnp.bfloat16)
    masked_again = masked_scores()
    prob_again = jnp.exp(masked_again - row_peak) / row_total
    prob_low = prob_again.astype(jnp.bfloat16)
    d_values = jnp.einsum("kgts,tkgd->skd", prob_low, d_att_low, preferred_element_type=jnp.float32)
    d_probs = jnp.einsum("tkgd,skd->kgts", d_att_low, v_group, preferred_element_type=jnp.float32)
    d_scores = (
        prob_again * (d_probs - jnp.sum(d_probs * prob_again, axis=-1, keepdims=True))
    ).astype(jnp.bfloat16)
    d_q_rot = (
        jnp.einsum("kgts,skd->tkgd", d_scores, k_low, preferred_element_type=jnp.float32)
        * score_scale
    )
    d_k_rot = (
        jnp.einsum("kgts,tkgd->skd", d_scores, q_low, preferred_element_type=jnp.float32)
        * score_scale
    )
    d_q_raw, d_k_raw = rope_back((d_q_rot.reshape(row_count, Q_HEADS, HEAD_DIM), d_k_rot))
    d_q_low = d_q_raw.astype(jnp.bfloat16)
    d_k_low = d_k_raw.astype(jnp.bfloat16)
    d_v_low = d_values.reshape(row_count, KD).astype(jnp.bfloat16)
    d_y_heads, d_x_post, d_z, g_skip = post_back(d_gated)
    d_y_low = d_y_heads.astype(jnp.bfloat16)
    d_mix = jnp.einsum("thp,shp->hts", d_y_low, vals_low, preferred_element_type=jnp.float32)
    d_vals = jnp.einsum("hts,thp->shp", mix_low, d_y_low, preferred_element_type=jnp.float32)
    d_gram = jnp.sum(d_mix * decay_mask, axis=0).astype(jnp.bfloat16)
    d_decay = d_mix * gram_cb[None]
    d_step = jnp.sum(d_vals * x_heads, axis=2)
    d_x_heads = d_x_post + d_vals * dt_step[:, :, None]
    d_c_state = jnp.dot(d_gram, b_low, preferred_element_type=jnp.float32)
    d_b_state = outer_sum(d_gram, c_low)
    d_xbc, d_dt_raw, g_conv_w, g_conv_b, g_dt_bias, g_a_log = pre_back(
        (d_x_heads, d_b_state, d_c_state, d_step, d_decay)
    )
    d_zxd = jnp.concatenate([d_z, d_xbc, d_dt_raw], axis=1).astype(jnp.bfloat16)
    d_proj = jnp.concatenate(
        [d_zxd, jnp.zeros((row_count, IN_PAD - DIN), jnp.bfloat16), d_q_low, d_k_low, d_v_low],
        axis=1,
    )
    d_normed = back_prod(d_proj, full_proj[:, :PROJ])
    d_resid, g_gain_a = norm_back_a(d_normed)
    d_tokens = (d_mid + d_resid).astype(jnp.bfloat16)
    flat = jnp.concatenate(
        [
            g_gain_a,
            g_gain_b,
            g_conv_w.reshape(-1),
            g_conv_b,
            g_dt_bias,
            g_a_log,
            g_skip,
        ]
    )
    small_rows = -(-flat.shape[0] // 1024) * 8
    small = jnp.pad(flat, (0, small_rows * 128 - flat.shape[0])).reshape(small_rows, 128)
    grads = (
        outer_sum(normed, d_proj).astype(jnp.bfloat16),
        outer_sum(d_branch, mixed_outs).astype(jnp.bfloat16),
        outer_sum(normed_b, d_glu).astype(jnp.bfloat16),
        outer_sum(cotangent, hidden).astype(jnp.bfloat16),
    )
    proj_rows, mixed_rows, glu_rows, down_rows, small_sum = reduce_grads(grads, small, n)
    sum_in = proj_rows[:, :DIN]
    sum_q = proj_rows[:, IN_PAD : IN_PAD + QD]
    sum_k = proj_rows[:, IN_PAD + QD : IN_PAD + QD + KD]
    sum_v = proj_rows[:, IN_PAD + QD + KD :]
    sum_o = mixed_rows[:, :QD].T
    sum_out = mixed_rows[:, QD:].T
    sum_gate = glu_rows[:, :FF]
    sum_up = glu_rows[:, FF:]
    sum_down = down_rows.T
    width = n * rows
    flat_sum = small_sum.reshape(-1)
    here = lax.axis_index("fsdp") * rows
    sum_gain_a = lax.dynamic_slice(flat_sum, (here,), (rows,))
    sum_gain_b = lax.dynamic_slice(flat_sum, (width + here,), (rows,))
    start = 2 * width
    pieces = []
    for size in (4 * CONV, CONV, 24, 24, 24):
        pieces.append(flat_sum[start : start + size])
        start += size
    sum_conv_w, sum_conv_b, sum_dt_bias, sum_a_log, sum_skip = pieces
    sum_conv_w = sum_conv_w.reshape(4, CONV)
    return (
        result,
        d_tokens,
        sum_in,
        sum_q,
        sum_k,
        sum_v,
        sum_o,
        sum_out,
        sum_gate,
        sum_up,
        sum_down,
        sum_gain_a,
        sum_gain_b,
        sum_conv_w,
        sum_conv_b,
        sum_dt_bias,
        sum_a_log,
        sum_skip,
    )


def solution(mesh):
    in_specs = (
        P("fsdp", None),
        P("fsdp", None),
        P("fsdp", None),
        P("fsdp", None),
        P("fsdp", None),
        P("fsdp", None),
        P("fsdp", None),
        P(None, "fsdp"),
        P(None, "fsdp"),
        P("fsdp", None),
        P("fsdp", None),
        P(None, "fsdp"),
        P("fsdp"),
        P("fsdp"),
        P(),
        P(),
        P(),
        P(),
        P(),
    )
    out_specs = (
        P("fsdp", None),
        P("fsdp", None),
        P("fsdp", None),
        P("fsdp", None),
        P("fsdp", None),
        P("fsdp", None),
        P(None, "fsdp"),
        P(None, "fsdp"),
        P("fsdp", None),
        P("fsdp", None),
        P(None, "fsdp"),
        P("fsdp"),
        P("fsdp"),
        P(),
        P(),
        P(),
        P(),
        P(),
    )
    return jax.shard_map(
        per_device, mesh=mesh, in_specs=in_specs, out_specs=out_specs, check_vma=False
    )
```

```python
import jax
import jax.numpy as jnp
from jax import lax
from jax.experimental import pallas as pl
from jax.experimental.pallas import tpu as pltpu
from jax.sharding import PartitionSpec as P

FF = 2048
STATE = 128
Q_HEADS = 8
KV_HEADS = 2
HEAD_DIM = 64
DSSM = 1536
CONV = 1792
DIN = 3352
QD = 512
KD = 128


norm_eps = 1e-05
rope_base = 100000000000.0


def segment_layout(lengths_row, row_count):
    seq_ends = jnp.cumsum(lengths_row)
    seq_starts = seq_ends - lengths_row
    places = jnp.arange(row_count, dtype=jnp.int32)
    segment = jnp.sum((places[:, None] >= seq_ends[None, :]).astype(jnp.int32), axis=1)
    picked = (
        segment[:, None] == jnp.arange(lengths_row.shape[0], dtype=jnp.int32)[None, :]
    ).astype(jnp.int32)
    position = places - jnp.sum(picked * seq_starts[None, :], axis=1)
    return (segment, position)


def rms_scaled(values, gain_row):
    return (
        values
        * lax.rsqrt(jnp.mean(values * values, axis=1, keepdims=True) + norm_eps)
        * gain_row[None, :]
    )


def rotate(values, position):
    half_dim = values.shape[-1] // 2
    ladder = jnp.arange(half_dim, dtype=jnp.float32) * (-2.0 / values.shape[-1])
    inverse = jnp.power(jnp.float32(rope_base), ladder)
    angles = position.astype(jnp.float32)[:, None] * inverse[None, :]
    cosine = jnp.cos(angles)[:, None, :]
    sine_rows = jnp.sin(angles)[:, None, :]
    half_one = values[..., :half_dim]
    second = values[..., half_dim:]
    return jnp.concatenate(
        [half_one * cosine - second * sine_rows, second * cosine + half_one * sine_rows], axis=-1
    )


def causal_conv(xbc_in, segment, conv_weight, conv_bias):
    row_count = xbc_in.shape[0]
    taps = conv_weight.shape[0]
    conv_sum = jnp.zeros_like(xbc_in) + conv_bias[None, :]
    for tap_index in range(taps):
        lag_rows = taps - 1 - tap_index
        shifted = jnp.pad(xbc_in, ((lag_rows, 0), (0, 0)))[:row_count]
        seg_shift = jnp.pad(segment, (lag_rows, 0), constant_values=-1)[:row_count]
        keep_rows = (seg_shift == segment).astype(xbc_in.dtype)
        conv_sum = conv_sum + conv_weight[tap_index][None, :] * shifted * keep_rows[:, None]
    return conv_sum


def mamba_inputs(xbc_in, dt_in, segment, conv_weight, conv_bias, dt_shift, a_logs):
    activated = jax.nn.silu(causal_conv(xbc_in, segment, conv_weight, conv_bias))
    row_count = xbc_in.shape[0]
    head_count = dt_shift.shape[0]
    x_heads = activated[:, :DSSM].reshape(row_count, head_count, DSSM // head_count)
    b_state = activated[:, DSSM : DSSM + STATE]
    c_state = activated[:, DSSM + STATE :]
    dt_step = jax.nn.softplus(dt_in + dt_shift[None, :])
    log_decay = -jnp.exp(a_logs)[None, :] * dt_step
    running = jnp.cumsum(log_decay, axis=0).T
    places = jnp.arange(row_count)
    causal = (segment[:, None] == segment[None, :]) & (places[:, None] >= places[None, :])
    gap_log = running[:, :, None] - running[:, None, :]
    decay_mask = jnp.exp(jnp.where(causal[None], gap_log, -10000.0))
    return (x_heads, b_state, c_state, dt_step, decay_mask)


def gated_out(y_heads, x_heads, z_gate, skip_rates):
    row_count = y_heads.shape[0]
    y_flat = (y_heads + skip_rates[None, :, None] * x_heads).reshape(row_count, -1)
    return y_flat * jax.nn.silu(z_gate)


def swiglu(gate_pre, upward):
    return jax.nn.silu(gate_pre) * upward


def forward_prod(rows_in, weight):
    return jnp.dot(rows_in, weight, preferred_element_type=jnp.float32)


def outer_sum(left_rows, right_rows):
    return lax.dot_general(
        left_rows, right_rows, (((0,), (0,)), ((), ())), preferred_element_type=jnp.float32
    )


def back_prod(grad_rows, weight):
    return lax.dot_general(
        grad_rows, weight, (((1,), (1,)), ((), ())), preferred_element_type=jnp.float32
    )


MESH = pl.DeviceIdType.MESH
IN_PAD = 3456
PROJ = IN_PAD + QD + 2 * KD
GATHER_CHUNKS = ((0, 0, 1024), (1, 0, 2048), (0, 1024, 3328), (2, 0, 2048), (2, 2048, 2048), (3, 0, 2048))
REDUCE_CHUNKS = ((3, 0, 2048), (2, 0, 2048), (2, 2048, 2048), (0, 0, 3200), (1, 0, 2048), (0, 3200, 1024))
AHEAD = 2


def place_of(me):
    return me // 8, (me // 4) % 2, (me // 2) % 2, me % 2


def index_of(z, y, x, core):
    return ((z * 2 + y) * 2 + x) * 2 + core


def enter(depth, z, y, x, core):
    barrier = pltpu.get_barrier_semaphore()
    partners = [
        index_of(z, y, x, 1 - core),
        index_of(z, y, 1 - x, core),
        index_of(z, 1 - y, x, core),
    ] + [index_of((z + j) % depth, y, x, core) for j in range(1, depth)]
    for partner in partners:
        pl.semaphore_signal(barrier, inc=1, device_id=(partner,), device_id_type=MESH)
    pl.semaphore_wait(barrier, len(partners))


def gather_kernel(depth, *refs):
    count = len(GATHER_CHUNKS)
    shards, fulls = refs[:4], refs[4:8]
    own_sem, z_send, z_recv, p_send, p_recv, c_send, c_recv = refs[8:]
    z, y, x, core = place_of(lax.axis_index("fsdp"))
    sibling = index_of(z, y, x, 1 - core)
    enter(depth, z, y, x, core)

    def remote(src, dst, send, recv, device):
        return pltpu.make_async_remote_copy(
            src_ref=src,
            dst_ref=dst,
            send_sem=send,
            recv_sem=recv,
            device_id=(device,),
            device_id_type=MESH,
        )

    own_copies, z_copies = [], []

    def start_z(c):
        which, first, width = GATHER_CHUNKS[c]
        cols = pl.ds(first, width)
        mine = shards[which].at[:, cols]
        spot = fulls[which].at[z, y, x, core, :, cols]
        row = []
        for j in range(1, depth):
            copy = remote(
                mine,
                spot,
                z_send.at[c, j - 1],
                z_recv.at[c, j - 1],
                index_of((z + j) % depth, y, x, core),
            )
            copy.start()
            row.append(copy)
        z_copies.append(row)
        own = pltpu.make_async_copy(mine, spot, own_sem.at[c])
        own.start()
        own_copies.append(own)

    for c in range(AHEAD):
        start_z(c)

    sent = []

    def region(c, ys, xs, co):
        which, first, width = GATHER_CHUNKS[c]
        return fulls[which].at[:, ys, xs, co, :, pl.ds(first, width)]

    def to_sibling(c, step, ys, xs):
        src = region(c, ys, xs, core)
        copy = remote(src, src, c_send.at[c, step], c_recv.at[c, step], sibling)
        copy.start()
        sent.append(copy)

    def step_one(c):
        which, first, width = GATHER_CHUNKS[c]
        for j in range(1, depth):
            spot = fulls[which].at[(z + depth - j) % depth, y, x, core, :, pl.ds(first, width)]
            remote(spot, spot, z_send.at[c, j - 1], z_recv.at[c, j - 1], sibling).wait_recv()
        own_copies[c].wait()
        if c + AHEAD < count:
            start_z(c + AHEAD)
        src = region(c, y, x, core)
        other = index_of(z, y, 1 - x, core) if c % 2 == 0 else index_of(z, 1 - y, x, core)
        copy = remote(src, src, p_send.at[c, 0], p_recv.at[c, 0], other)
        copy.start()
        sent.append(copy)
        to_sibling(c, 0, y, x)

    def step_two(c):
        if c % 2 == 0:
            spot = region(c, y, 1 - x, core)
            src = region(c, y, slice(None), core)
            other = index_of(z, 1 - y, x, core)
        else:
            spot = region(c, 1 - y, x, core)
            src = region(c, slice(None), x, core)
            other = index_of(z, y, 1 - x, core)
        remote(spot, spot, p_send.at[c, 0], p_recv.at[c, 0], sibling).wait_recv()
        copy = remote(src, src, p_send.at[c, 1], p_recv.at[c, 1], other)
        copy.start()
        sent.append(copy)
        if c % 2 == 0:
            to_sibling(c, 1, y, 1 - x)
        else:
            to_sibling(c, 1, 1 - y, x)

    def step_three(c):
        if c % 2 == 0:
            ys, xs = 1 - y, slice(None)
        else:
            ys, xs = slice(None), 1 - x
        spot = region(c, ys, xs, core)
        remote(spot, spot, p_send.at[c, 1], p_recv.at[c, 1], sibling).wait_recv()
        to_sibling(c, 2, ys, xs)

    for t in range(count + 2):
        if t < count:
            step_one(t)
        if 0 <= t - 1 < count:
            step_two(t - 1)
        if 0 <= t - 2 < count:
            step_three(t - 2)
    for c in range(count):
        if c % 2 == 0:
            parts = ((y, x), (y, 1 - x), (1 - y, slice(None)))
        else:
            parts = ((y, x), (1 - y, x), (slice(None), 1 - x))
        for step, (ys, xs) in enumerate(parts):
            spot = region(c, ys, xs, 1 - core)
            remote(spot, spot, c_send.at[c, step], c_recv.at[c, step], sibling).wait_recv()
    for row in z_copies:
        for copy in row:
            copy.wait_send()
    for copy in sent:
        copy.wait_send()


def gather_fast(shards, n):
    depth = n // 8
    rows = shards[0].shape[0]
    count = len(GATHER_CHUNKS)
    anywhere = pl.BlockSpec(memory_space=pl.ANY)
    dma = pltpu.SemaphoreType.DMA
    fulls = pl.pallas_call(
        lambda *refs: gather_kernel(depth, *refs),
        out_shape=tuple(
            jax.ShapeDtypeStruct((depth, 2, 2, 2, rows, s.shape[1]), s.dtype) for s in shards
        ),
        in_specs=[anywhere] * 4,
        out_specs=(anywhere,) * 4,
        scratch_shapes=[
            dma((count,)),
            dma((count, depth - 1)),
            dma((count, depth - 1)),
            dma((count, 2)),
            dma((count, 2)),
            dma((count, 3)),
            dma((count, 3)),
        ],
        compiler_params=pltpu.CompilerParams(collective_id=0, has_side_effects=True),
        name="gather_weights",
    )(*shards)
    return tuple(f.reshape(n * rows, f.shape[-1]) for f in fulls)


def reduce_kernel(depth, *refs):
    count = len(REDUCE_CHUNKS)
    grads, small = refs[:4], refs[4]
    outs, small_out = refs[5:9], refs[9]
    rest = list(refs[10:])
    held = rest[:count]
    c_buf = rest[count : 2 * count]
    one_buf = rest[2 * count : 3 * count]
    two_buf = rest[3 * count : 4 * count]
    z_buf = rest[4 * count : 5 * count]
    (s_cur, s_buf, s_z, own_sem, c_send, c_recv, p_send, p_recv, z_send, z_recv,
     s_send, s_recv, sz_send, sz_recv) = rest[5 * count :]
    z, y, x, core = place_of(lax.axis_index("fsdp"))
    sibling = index_of(z, y, x, 1 - core)
    beside_x = index_of(z, y, 1 - x, core)
    beside_y = index_of(z, 1 - y, x, core)
    enter(depth, z, y, x, core)

    def remote(src, dst, send, recv, device):
        return pltpu.make_async_remote_copy(
            src_ref=src,
            dst_ref=dst,
            send_sem=send,
            recv_sem=recv,
            device_id=(device,),
            device_id_type=MESH,
        )

    core_copies, own_copies, sent = [], [], []

    def start_core(c):
        which, first, width = REDUCE_CHUNKS[c]
        cols = pl.ds(first, width)
        copy = remote(
            grads[which].at[:, :, :, 1 - core, :, cols],
            c_buf[c],
            c_send.at[c],
            c_recv.at[c],
            sibling,
        )
        copy.start()
        core_copies.append(copy)
        own = pltpu.make_async_copy(
            grads[which].at[:, :, :, core, :, cols], held[c], own_sem.at[c]
        )
        own.start()
        own_copies.append(own)

    for c in range(AHEAD):
        start_core(c)

    def summed(first, second):
        return (first.astype(jnp.float32) + second.astype(jnp.float32)).astype(jnp.bfloat16)

    def step_core(c):
        own_copies[c].wait()
        core_copies[c].wait_recv()
        if c + AHEAD < count:
            start_core(c + AHEAD)

        def add(i, carry):
            a, b, d = i // 4, (i // 2) % 2, i % 2
            held[c][a, b, d] = summed(held[c][a, b, d], c_buf[c][a, b, d])
            return carry

        lax.fori_loop(0, depth * 4, add, 0)
        if c % 2 == 0:
            copy = remote(
                held[c].at[:, 1 - y], one_buf[c], p_send.at[c, 0], p_recv.at[c, 0], beside_y
            )
        else:
            copy = remote(
                held[c].at[:, :, 1 - x], one_buf[c], p_send.at[c, 0], p_recv.at[c, 0], beside_x
            )
        copy.start()
        sent.append(copy)

    def step_one(c):
        remote(one_buf[c], one_buf[c], p_send.at[c, 0], p_recv.at[c, 0], sibling).wait_recv()

        def add(i, carry):
            a, b = i // 2, i % 2
            if c % 2 == 0:
                held[c][a, y, b] = summed(held[c][a, y, b], one_buf[c][a, b])
            else:
                held[c][a, b, x] = summed(held[c][a, b, x], one_buf[c][a, b])
            return carry

        lax.fori_loop(0, depth * 2, add, 0)
        if c % 2 == 0:
            src, other = held[c].at[:, y, 1 - x], beside_x
        else:
            src, other = held[c].at[:, 1 - y, x], beside_y
        copy = remote(src, two_buf[c], p_send.at[c, 1], p_recv.at[c, 1], other)
        copy.start()
        sent.append(copy)

    def step_two(c):
        remote(two_buf[c], two_buf[c], p_send.at[c, 1], p_recv.at[c, 1], sibling).wait_recv()

        def add(a, carry):
            held[c][a, y, x] = summed(held[c][a, y, x], two_buf[c][a])
            return carry

        lax.fori_loop(0, depth, add, 0)
        for j in range(1, depth):
            to = (z + j) % depth
            copy = remote(
                held[c].at[to, y, x],
                z_buf[c].at[j - 1],
                z_send.at[c, j - 1],
                z_recv.at[c, j - 1],
                index_of(to, y, x, core),
            )
            copy.start()
            sent.append(copy)

    def step_z(c):
        which, first, width = REDUCE_CHUNKS[c]
        total = held[c][z, y, x].astype(jnp.float32)
        for j in range(1, depth):
            spot = z_buf[c].at[j - 1]
            remote(spot, spot, z_send.at[c, j - 1], z_recv.at[c, j - 1], sibling).wait_recv()
            total = total + z_buf[c][j - 1].astype(jnp.float32)
        outs[which][:, first : first + width] = total

    small_sent = []

    def small_start(step):
        if step == 0:
            s_cur[...] = small[...]
        if step < 3:
            copy = remote(
                s_cur,
                s_buf.at[step],
                s_send.at[step],
                s_recv.at[step],
                (sibling, beside_x, beside_y)[step],
            )
            copy.start()
            small_sent.append(copy)
        else:
            s_z[z] = s_cur[...]
            for j in range(1, depth):
                copy = remote(
                    s_cur,
                    s_z.at[z],
                    sz_send.at[j - 1],
                    sz_recv.at[j - 1],
                    index_of((z + j) % depth, y, x, core),
                )
                copy.start()
                sent.append(copy)

    def small_end(step):
        if step < 3:
            small_sent[step].wait()
            s_cur[...] = s_cur[...] + s_buf[step]
        else:
            for j in range(1, depth):
                spot = s_z.at[(z + depth - j) % depth]
                remote(spot, spot, sz_send.at[j - 1], sz_recv.at[j - 1], sibling).wait_recv()
            total = s_z[0]
            for a in range(1, depth):
                total = total + s_z[a]
            small_out[...] = total

    small_start(0)
    for t in range(count + 3):
        if t < count:
            step_core(t)
        if 0 <= t - 1 < count:
            step_one(t - 1)
        if 0 <= t - 2 < count:
            step_two(t - 2)
        if 0 <= t - 3 < count:
            step_z(t - 3)
        if t < 4:
            small_end(t)
        if t < 3:
            small_start(t + 1)
    for copy in core_copies:
        copy.wait_send()
    for copy in sent:
        copy.wait_send()


def reduce_fast(grads, small, n):
    depth = n // 8
    rows = grads[0].shape[0] // n
    count = len(REDUCE_CHUNKS)
    anywhere = pl.BlockSpec(memory_space=pl.ANY)
    vmem = pl.BlockSpec(memory_space=pltpu.VMEM)
    dma = pltpu.SemaphoreType.DMA
    blocks = [g.reshape(depth, 2, 2, 2, rows, g.shape[1]) for g in grads]
    widths = [width for (_, _, width) in REDUCE_CHUNKS]

    def buffers(*lead):
        return [pltpu.VMEM(lead + (rows, width), jnp.bfloat16) for width in widths]

    return pl.pallas_call(
        lambda *refs: reduce_kernel(depth, *refs),
        out_shape=tuple(jax.ShapeDtypeStruct((rows, g.shape[1]), jnp.float32) for g in grads)
        + (jax.ShapeDtypeStruct(small.shape, jnp.float32),),
        in_specs=[anywhere] * 4 + [vmem],
        out_specs=(vmem,) * 5,
        scratch_shapes=buffers(depth, 2, 2)
        + buffers(depth, 2, 2)
        + buffers(depth, 2)
        + buffers(depth)
        + buffers(depth - 1)
        + [
            pltpu.VMEM(small.shape, jnp.float32),
            pltpu.VMEM((3,) + small.shape, jnp.float32),
            pltpu.VMEM((depth,) + small.shape, jnp.float32),
            dma((count,)),
            dma((count,)),
            dma((count,)),
            dma((count, 2)),
            dma((count, 2)),
            dma((count, depth - 1)),
            dma((count, depth - 1)),
            dma((3,)),
            dma((3,)),
            dma((depth - 1,)),
            dma((depth - 1,)),
        ],
        compiler_params=pltpu.CompilerParams(
            collective_id=1, has_side_effects=True, vmem_limit_bytes=52 * 1024 * 1024
        ),
        name="reduce_grads",
    )(*blocks, small)


def gather_weights(shards, n):
    if n == 32:
        return gather_fast(shards, n)
    return tuple(lax.all_gather(s, "fsdp", axis=0, tiled=True) for s in shards)


def reduce_grads(grads, small, n):
    if n == 32:
        return reduce_fast(grads, small, n)
    summed = [
        lax.psum_scatter(g.astype(jnp.float32), "fsdp", scatter_dimension=0, tiled=True)
        for g in grads
    ]
    return (*summed, lax.psum(small, "fsdp"))


def per_device(
    tokens,
    lengths,
    cotangent,
    w_in,
    w_q,
    w_k,
    w_v,
    w_o,
    w_out,
    w_gate,
    w_up,
    w_down,
    gain_a,
    gain_b,
    conv_w,
    conv_b,
    dt_bias,
    a_log,
    d_skip,
):
    n = lax.axis_size("fsdp")
    rows = w_in.shape[0]

    def blank(columns):
        return jnp.zeros((rows, columns), jnp.bfloat16)

    shards = (
        jnp.concatenate(
            [
                w_in,
                blank(IN_PAD - DIN),
                w_q,
                w_k,
                w_v,
                gain_a[:, None],
                gain_b[:, None],
                blank(126),
            ],
            axis=1,
        ),
        jnp.concatenate([w_o.T, w_out.T], axis=1),
        jnp.concatenate([w_gate, w_up], axis=1),
        w_down.T,
    )
    full_proj, full_mixed, full_glu, full_down = gather_weights(shards, n)
    full_ga = full_proj[:, PROJ]
    full_gb = full_proj[:, PROJ + 1]
    row_count = tokens.shape[0]
    segment, position = segment_layout(lengths[0], row_count)
    places = jnp.arange(row_count)
    causal = (segment[:, None] == segment[None, :]) & (places[:, None] >= places[None, :])
    resid_in = tokens.astype(jnp.float32)
    normed_f, norm_back_a = jax.vjp(rms_scaled, resid_in, full_ga.astype(jnp.float32))
    normed = normed_f.astype(jnp.bfloat16)
    projected = forward_prod(normed, full_proj)
    zxd = projected[:, :DIN]
    q_raw = projected[:, IN_PAD : IN_PAD + QD]
    k_raw = projected[:, IN_PAD + QD : IN_PAD + QD + KD]
    v_low = projected[:, IN_PAD + QD + KD : PROJ].astype(jnp.bfloat16)
    z_gate = zxd[:, :DSSM]
    xbc_in = zxd[:, DSSM : DSSM + CONV]
    dt_raw = zxd[:, DSSM + CONV :]

    def pre_part(xbc_part, dt_part, conv_weight, conv_bias, dt_shift, a_logs):
        return mamba_inputs(xbc_part, dt_part, segment, conv_weight, conv_bias, dt_shift, a_logs)

    (x_heads, b_state, c_state, dt_step, decay_mask), pre_back = jax.vjp(
        pre_part, xbc_in, dt_raw, conv_w, conv_b, dt_bias, a_log
    )
    b_low = b_state.astype(jnp.bfloat16)
    c_low = c_state.astype(jnp.bfloat16)
    gram_cb = lax.dot_general(
        c_low, b_low, (((1,), (1,)), ((), ())), preferred_element_type=jnp.float32
    )
    mix_low = (gram_cb[None] * decay_mask).astype(jnp.bfloat16)
    vals_low = (dt_step[:, :, None] * x_heads).astype(jnp.bfloat16)
    y_heads = jnp.einsum("hts,shp->thp", mix_low, vals_low, preferred_element_type=jnp.float32)
    gated_f, post_back = jax.vjp(gated_out, y_heads, x_heads, z_gate, d_skip)
    gated_low = gated_f.astype(jnp.bfloat16)

    def rope_pair(q_part, k_part):
        return (
            rotate(q_part.reshape(row_count, Q_HEADS, HEAD_DIM), position),
            rotate(k_part.reshape(row_count, KV_HEADS, HEAD_DIM), position),
        )

    (q_rot, k_rot), rope_back = jax.vjp(rope_pair, q_raw, k_raw)
    group_size = Q_HEADS // KV_HEADS
    q_low = q_rot.astype(jnp.bfloat16).reshape(row_count, KV_HEADS, group_size, HEAD_DIM)
    k_low = k_rot.astype(jnp.bfloat16)
    v_group = v_low.reshape(row_count, KV_HEADS, HEAD_DIM)
    score_scale = HEAD_DIM ** (-0.5)

    def masked_scores():
        raw_scores = (
            jnp.einsum("tkgd,skd->kgts", q_low, k_low, preferred_element_type=jnp.float32)
            * score_scale
        )
        return jnp.where(causal[None, None], raw_scores, -1000000000.0)

    masked = masked_scores()
    row_peak = jnp.max(masked, axis=-1, keepdims=True)
    row_total = jnp.sum(jnp.exp(masked - row_peak), axis=-1, keepdims=True)
    prob_rows = jnp.exp(masked - row_peak) / row_total
    attended = jnp.einsum(
        "kgts,skd->tkgd",
        prob_rows.astype(jnp.bfloat16),
        v_group,
        preferred_element_type=jnp.float32,
    )
    context = attended.astype(jnp.bfloat16).reshape(row_count, QD)
    mixed_outs = jnp.concatenate([context, gated_low], axis=1)
    mid_sum = resid_in + back_prod(mixed_outs, full_mixed)
    normed_bf, norm_back_b = jax.vjp(rms_scaled, mid_sum, full_gb.astype(jnp.float32))
    normed_b = normed_bf.astype(jnp.bfloat16)
    glu_pre = forward_prod(normed_b, full_glu)
    gate_pre = glu_pre[:, :FF]
    upward = glu_pre[:, FF:]
    hidden_f, glu_back = jax.vjp(swiglu, gate_pre, upward)
    hidden = hidden_f.astype(jnp.bfloat16)
    result = (mid_sum + back_prod(hidden, full_down)).astype(jnp.bfloat16)
    grad_top = cotangent.astype(jnp.float32)
    d_hidden = forward_prod(cotangent, full_down)
    d_gate_f, d_up_f = glu_back(d_hidden)
    d_gate = d_gate_f.astype(jnp.bfloat16)
    d_up = d_up_f.astype(jnp.bfloat16)
    d_glu = jnp.concatenate([d_gate, d_up], axis=1)
    d_normed_b = back_prod(d_glu, full_glu)
    d_mid_norm, g_gain_b = norm_back_b(d_normed_b)
    d_mid = grad_top + d_mid_norm
    d_branch = d_mid.astype(jnp.bfloat16)
    d_mixed = forward_prod(d_branch, full_mixed)
    d_context = d_mixed[:, :QD]
    d_gated = d_mixed[:, QD:]
    d_att_low = d_context.reshape(row_count, KV_HEADS, group_size, HEAD_DIM).astype(jnp.bfloat16)
    masked_again = masked_scores()
    prob_again = jnp.exp(masked_again - row_peak) / row_total
    prob_low = prob_again.astype(jnp.bfloat16)
    d_values = jnp.einsum("kgts,tkgd->skd", prob_low, d_att_low, preferred_element_type=jnp.float32)
    d_probs = jnp.einsum("tkgd,skd->kgts", d_att_low, v_group, preferred_element_type=jnp.float32)
    d_scores = (
        prob_again * (d_probs - jnp.sum(d_probs * prob_again, axis=-1, keepdims=True))
    ).astype(jnp.bfloat16)
    d_q_rot = (
        jnp.einsum("kgts,skd->tkgd", d_scores, k_low, preferred_element_type=jnp.float32)
        * score_scale
    )
    d_k_rot = (
        jnp.einsum("kgts,tkgd->skd", d_scores, q_low, preferred_element_type=jnp.float32)
        * score_scale
    )
    d_q_raw, d_k_raw = rope_back((d_q_rot.reshape(row_count, Q_HEADS, HEAD_DIM), d_k_rot))
    d_q_low = d_q_raw.astype(jnp.bfloat16)
    d_k_low = d_k_raw.astype(jnp.bfloat16)
    d_v_low = d_values.reshape(row_count, KD).astype(jnp.bfloat16)
    d_y_heads, d_x_post, d_z, g_skip = post_back(d_gated)
    d_y_low = d_y_heads.astype(jnp.bfloat16)
    d_mix = jnp.einsum("thp,shp->hts", d_y_low, vals_low, preferred_element_type=jnp.float32)
    d_vals = jnp.einsum("hts,thp->shp", mix_low, d_y_low, preferred_element_type=jnp.float32)
    d_gram = jnp.sum(d_mix * decay_mask, axis=0).astype(jnp.bfloat16)
    d_decay = d_mix * gram_cb[None]
    d_step = jnp.sum(d_vals * x_heads, axis=2)
    d_x_heads = d_x_post + d_vals * dt_step[:, :, None]
    d_c_state = jnp.dot(d_gram, b_low, preferred_element_type=jnp.float32)
    d_b_state = outer_sum(d_gram, c_low)
    d_xbc, d_dt_raw, g_conv_w, g_conv_b, g_dt_bias, g_a_log = pre_back(
        (d_x_heads, d_b_state, d_c_state, d_step, d_decay)
    )
    d_zxd = jnp.concatenate([d_z, d_xbc, d_dt_raw], axis=1).astype(jnp.bfloat16)
    d_proj = jnp.concatenate(
        [d_zxd, jnp.zeros((row_count, IN_PAD - DIN), jnp.bfloat16), d_q_low, d_k_low, d_v_low],
        axis=1,
    )
    d_normed = back_prod(d_proj, full_proj[:, :PROJ])
    d_resid, g_gain_a = norm_back_a(d_normed)
    d_tokens = (d_mid + d_resid).astype(jnp.bfloat16)
    flat = jnp.concatenate(
        [
            g_gain_a,
            g_gain_b,
            g_conv_w.reshape(-1),
            g_conv_b,
            g_dt_bias,
            g_a_log,
            g_skip,
        ]
    )
    small_rows = -(-flat.shape[0] // 1024) * 8
    small = jnp.pad(flat, (0, small_rows * 128 - flat.shape[0])).reshape(small_rows, 128)
    grads = (
        outer_sum(normed, d_proj).astype(jnp.bfloat16),
        outer_sum(d_branch, mixed_outs).astype(jnp.bfloat16),
        outer_sum(normed_b, d_glu).astype(jnp.bfloat16),
        outer_sum(cotangent, hidden).astype(jnp.bfloat16),
    )
    proj_rows, mixed_rows, glu_rows, down_rows, small_sum = reduce_grads(grads, small, n)
    sum_in = proj_rows[:, :DIN]
    sum_q = proj_rows[:, IN_PAD : IN_PAD + QD]
    sum_k = proj_rows[:, IN_PAD + QD : IN_PAD + QD + KD]
    sum_v = proj_rows[:, IN_PAD + QD + KD :]
    sum_o = mixed_rows[:, :QD].T
    sum_out = mixed_rows[:, QD:].T
    sum_gate = glu_rows[:, :FF]
    sum_up = glu_rows[:, FF:]
    sum_down = down_rows.T
    width = n * rows
    flat_sum = small_sum.reshape(-1)
    here = lax.axis_index("fsdp") * rows
    sum_gain_a = lax.dynamic_slice(flat_sum, (here,), (rows,))
    sum_gain_b = lax.dynamic_slice(flat_sum, (width + here,), (rows,))
    start = 2 * width
    pieces = []
    for size in (4 * CONV, CONV, 24, 24, 24):
        pieces.append(flat_sum[start : start + size])
        start += size
    sum_conv_w, sum_conv_b, sum_dt_bias, sum_a_log, sum_skip = pieces
    sum_conv_w = sum_conv_w.reshape(4, CONV)
    return (
        result,
        d_tokens,
        sum_in,
        sum_q,
        sum_k,
        sum_v,
        sum_o,
        sum_out,
        sum_gate,
        sum_up,
        sum_down,
        sum_gain_a,
        sum_gain_b,
        sum_conv_w,
        sum_conv_b,
        sum_dt_bias,
        sum_a_log,
        sum_skip,
    )


def solution(mesh):
    in_specs = (
        P("fsdp", None),
        P("fsdp", None),
        P("fsdp", None),
        P("fsdp", None),
        P("fsdp", None),
        P("fsdp", None),
        P("fsdp", None),
        P(None, "fsdp"),
        P(None, "fsdp"),
        P("fsdp", None),
        P("fsdp", None),
        P(None, "fsdp"),
        P("fsdp"),
        P("fsdp"),
        P(),
        P(),
        P(),
        P(),
        P(),
    )
    out_specs = (
        P("fsdp", None),
        P("fsdp", None),
        P("fsdp", None),
        P("fsdp", None),
        P("fsdp", None),
        P("fsdp", None),
        P(None, "fsdp"),
        P(None, "fsdp"),
        P("fsdp", None),
        P("fsdp", None),
        P(None, "fsdp"),
        P("fsdp"),
        P("fsdp"),
        P(),
        P(),
        P(),
        P(),
        P(),
    )
    return jax.shard_map(
        per_device, mesh=mesh, in_specs=in_specs, out_specs=out_specs, check_vma=False
    )
```
